32 devices in a mesh: agg: 8 (over y, x, core), grp: 4 (over z).
Axes of the slice: x: 2, y: 2, z: 4, core: 2. Of those that a mesh axis runs over, the one named last changes fastest.
Arguments:
- a_blocks: bfloat16 [8, 4, 16, 5, 128, 128], P('agg', 'grp'), may hold values from -0.5 to 0.5
- a_cols: int32 [8, 4, 16, 5], P('agg', 'grp'), may hold values from 0 to 23, as said below
- p_blocks: bfloat16 [8, 4, 16, 2, 128, 128], P('agg', 'grp'), may hold values from -0.5 to 0.5
- p_cols: int32 [8, 4, 16, 2], P(None, 'grp'), may hold values from 0 to 2, as said below
Outputs:
- coarse_matrix: bfloat16 [8, 128, 3, 9, 128], P('agg')
The draws below stay inside these ranges and needn't reach their ends.
Inputs may be any that keep to these rules, and one draw needn't show every extreme that they name: `a_cols`: slot 0 of row r is 4 + r. In every region but the first, slot 1 of the rows r < 4 names a row 0 to 4 - 1 (row 0 names 0); in every region but the last, slot 4 of the rows r >= 12 names a row 20 to 16 + 2 * 4 - 1 (row 15 names the last). All other slots name rows 4 to 19; a row may name a column more than once. `p_cols`: the 2 entries of a row are 2 consecutive coarse rows counted modulo 3, all different. Every index of agg holds the whole array.
All inputs are finite; a program needn't handle non-finite values.
Results may differ from the reference program's by a relative error of at most 0.025.
Values may be sent and summed in bfloat16 or wider, within the bound.
A program may use at most 64 MiB of HBM per device.

```python
import jax
import jax.numpy as jnp
from jax import lax

B = 128
FR = 16
KA = 5
KP = 2
NC = 3
HB = 4
REGIONS = 8
MEMBERS = 4


def draw_a_cols(key, part):
    full_shape = (REGIONS, MEMBERS, FR, KA)
    own_rows = HB + jax.random.randint(jax.random.fold_in(key, 11), full_shape, 0, FR)
    behind_rows = jax.random.randint(jax.random.fold_in(key, 12), full_shape, 0, HB)
    ahead_rows = HB + FR + jax.random.randint(jax.random.fold_in(key, 13), full_shape, 0, HB)
    region_index = lax.broadcasted_iota(jnp.int32, full_shape, 0)
    row_index = lax.broadcasted_iota(jnp.int32, full_shape, 2)
    slot_index = lax.broadcasted_iota(jnp.int32, full_shape, 3)
    behind_rows = jnp.where(row_index == 0, 0, behind_rows)
    ahead_rows = jnp.where(row_index == FR - 1, FR + 2 * HB - 1, ahead_rows)
    columns = jnp.where(slot_index == 0, HB + row_index, own_rows)
    columns = jnp.where((slot_index == 1) & (row_index < HB) & (region_index > 0), behind_rows, columns)
    columns = jnp.where((slot_index == KA - 1) & (row_index >= FR - HB) & (region_index < REGIONS - 1), ahead_rows, columns)
    return columns.astype(jnp.int32)


def draw_p_cols(key, part):
    full_shape = (REGIONS, MEMBERS, FR, KP)
    offsets = jax.random.randint(jax.random.fold_in(key, 21), (REGIONS, MEMBERS, FR, 1), 0, NC)
    first_index = lax.broadcasted_iota(jnp.int32, (REGIONS, MEMBERS, FR, 1), 0)
    second_index = lax.broadcasted_iota(jnp.int32, (REGIONS, MEMBERS, FR, 1), 1)
    third_index = lax.broadcasted_iota(jnp.int32, (REGIONS, MEMBERS, FR, 1), 2)
    leading = (first_index == 0) & (second_index == 0) & (third_index == 0)
    offsets = jnp.where(leading, NC - 1, offsets)
    slot_index = lax.broadcasted_iota(jnp.int32, full_shape, 3)
    return ((offsets + slot_index) % NC).astype(jnp.int32)


def block_scale(rng, dims, cuts, least, largest):
    gain, own = 1.0, jax.random.fold_in(rng, 6)
    for position, shards_of in cuts:
        steps = jnp.exp(jax.random.uniform(jax.random.fold_in(own, position), (shards_of,), jnp.float32, least / len(cuts), largest / len(cuts)))
        gain = gain * jnp.repeat(steps, dims[position] // shards_of).reshape([-1 if axis == position else 1 for axis in range(len(dims))])
    return gain


def centred(key, shape, deviation, bound, cuts=(), kind=jnp.bfloat16):
    gain = block_scale(key, shape, cuts, -0.22, 0.18) if cuts else 1.0
    entries = jax.random.normal(key, shape, jnp.float32) * deviation * gain
    return jnp.minimum(jnp.maximum(entries, -bound), bound).astype(kind)


def setup_inputs(seed: int = 0) -> dict:
    keys = jax.random.split(jax.random.key(seed), 5)
    a_blocks = centred(keys[0], (REGIONS, MEMBERS, FR, KA, B, B), B ** -0.5, 0.5, ((0, 8), (1, 4)))
    a_cols = draw_a_cols(jax.random.fold_in(keys[4], 71), 0)
    p_blocks = centred(keys[2], (REGIONS, MEMBERS, FR, KP, B, B), B ** -0.5, 0.5, ((0, 8), (1, 4)))
    p_cols = draw_p_cols(jax.random.fold_in(keys[4], 71), 0)
    return dict(a_blocks=a_blocks, a_cols=a_cols, p_blocks=p_blocks, p_cols=p_cols)


def device_term(a_here, col_here, p_ext_here, ids_ext_here, p_here, pc_here):
    band = 3 * NC
    targets = NC * band
    taken = p_ext_here[col_here]
    applied = jnp.einsum('rkxy,rkmyz->rkmxz', a_here.astype(jnp.float32), taken.astype(jnp.float32))
    applied = applied.astype(jnp.bfloat16).reshape(FR, KA * KP, B, B)
    slot_ids = ids_ext_here[col_here].reshape(FR, KA * KP)
    pieces = jnp.einsum('rnxy,rsxz->rnsyz', p_here.astype(jnp.float32), applied.astype(jnp.float32))
    target_ids = (pc_here[:, :, None] * band + slot_ids[:, None, :]).reshape(-1).astype(jnp.int32)
    summed = jax.ops.segment_sum(pieces.reshape(-1, B, B), target_ids, num_segments=targets)
    rounded = lax.optimization_barrier(summed.astype(jnp.bfloat16))
    return rounded.astype(jnp.float32)


def reference(a_blocks, a_cols, p_blocks, p_cols):
    band = 3 * NC
    targets = NC * band
    zero_rim = jnp.zeros((1, MEMBERS, HB, KP, B, B), p_blocks.dtype)
    behind = jnp.concatenate([zero_rim, p_blocks[:-1, :, FR - HB:]], 0)
    ahead = jnp.concatenate([p_blocks[1:, :, :HB], zero_rim], 0)
    p_extended = jnp.concatenate([behind, p_blocks, ahead], 2)
    zero_ids = jnp.zeros((1, MEMBERS, HB, KP), jnp.int32)
    ids_behind = jnp.concatenate([zero_ids, p_cols[:-1, :, FR - HB:]], 0)
    ids_ahead = jnp.concatenate([p_cols[1:, :, :HB], zero_ids], 0) + 2 * NC
    ids_extended = jnp.concatenate([ids_behind, p_cols + NC, ids_ahead], 2).astype(jnp.int32)

    def region_matrix(index):
        def add_member(total, member):
            term = device_term(a_blocks[index][member], a_cols[index][member], p_extended[index][member], ids_extended[index][member], p_blocks[index][member], p_cols[index][member])
            return total + term, None

        total, _ = lax.scan(add_member, jnp.zeros((targets, B, B), jnp.float32), jnp.arange(MEMBERS, dtype=jnp.int32))
        return total.astype(jnp.bfloat16).transpose(1, 0, 2).reshape(B, NC, band, B)

    return lax.map(region_matrix, jnp.arange(REGIONS, dtype=jnp.int32))
```

```python
import functools

import jax
import jax.numpy as jnp
from jax import lax
from jax.experimental import pallas as pl
from jax.experimental.pallas import tpu as pltpu
from jax.sharding import PartitionSpec as P

NC = 3
HB = 4
LAG = 4
GROUP = 4
MESH = pl.DeviceIdType.MESH
BF = jnp.bfloat16
F32 = jnp.float32


def kernel(
    regions,
    members,
    a_ref,
    ac_ref,
    p_ref,
    pc_ref,
    out_ref,
    a_v,
    p_v,
    halo_lo,
    halo_hi,
    e_own,
    e_lo,
    e_hi,
    et,
    g_own,
    g_lo,
    g_hi,
    term,
    half,
    from_outer,
    from_inner,
    a_sem,
    p_sem,
    lo_send,
    lo_recv,
    hi_send,
    hi_recv,
    up_send,
    up_recv,
    down_send,
    down_recv,
    out_sem,
):
    rows, slots, width = a_v.shape[0], a_v.shape[1], a_v.shape[2]
    wide = NC * width
    band = 3 * NC
    count = NC * band
    region = lax.axis_index("agg")
    g = lax.axis_index("grp")
    first = region == 0
    last = region == regions - 1
    left = g < members // 2
    inner = jnp.where(left, g + 1, g - 1)
    outer = jnp.where(left, g - 1, g + 1)
    has_outer = jnp.logical_and(g > 0, g < members - 1)
    is_end = jnp.logical_not(has_outer)
    is_mid = jnp.logical_or(g == members // 2 - 1, g == members // 2)

    p_copy = pltpu.make_async_copy(p_ref.at[0, 0], p_v, p_sem)
    p_copy.start()

    def a_copy(i):
        return pltpu.make_async_copy(
            a_ref.at[0, 0, pl.ds(i * GROUP, GROUP)],
            a_v.at[pl.ds(i * GROUP, GROUP)],
            a_sem.at[i],
        )

    for i in range(rows // GROUP):
        a_copy(i).start()

    barrier = pltpu.get_barrier_semaphore()

    def greet(there, agg, grp):
        @pl.when(there)
        def _():
            pl.semaphore_signal(barrier, inc=1, device_id=(agg, grp), device_id_type=MESH)

    greet(jnp.logical_not(first), region - 1, g)
    greet(jnp.logical_not(last), region + 1, g)
    greet(has_outer, region, outer)
    greet(jnp.bool_(True), region, inner)
    pl.semaphore_wait(
        barrier,
        1
        + has_outer.astype(jnp.int32)
        + jnp.logical_not(first).astype(jnp.int32)
        + jnp.logical_not(last).astype(jnp.int32),
    )

    def to_next():
        return pltpu.make_async_remote_copy(
            src_ref=p_ref.at[0, 0, pl.ds(rows - HB, HB)],
            dst_ref=halo_lo,
            send_sem=lo_send,
            recv_sem=lo_recv,
            device_id=(region + 1, g),
            device_id_type=MESH,
        )

    def to_previous():
        return pltpu.make_async_remote_copy(
            src_ref=p_ref.at[0, 0, pl.ds(0, HB)],
            dst_ref=halo_hi,
            send_sem=hi_send,
            recv_sem=hi_recv,
            device_id=(region - 1, g),
            device_id_type=MESH,
        )

    @pl.when(jnp.logical_not(last))
    def _():
        to_next().start()

    @pl.when(jnp.logical_not(first))
    def _():
        to_previous().start()

    def placed(block_0, block_1, id_0, id_1):
        zero = jnp.zeros_like(block_0)
        return jnp.concatenate(
            [
                jnp.where(id_0 == c, block_0, jnp.where(id_1 == c, block_1, zero))
                for c in range(NC)
            ],
            axis=1,
        )

    p_copy.wait()

    def build(r, carry):
        row = placed(p_v[r, 0], p_v[r, 1], pc_ref[region, 0, r, 0], pc_ref[region, 0, r, 1])
        e_own[r] = row
        et[:, pl.ds(pl.multiple_of(r * width, width), width)] = row.T
        return carry

    lax.fori_loop(0, rows, build, 0, unroll=4)

    def multiply(i, carry):
        a_copy(i).wait()
        for j in range(GROUP):
            r = i * GROUP + j
            pieces = []
            for k in range(slots):
                col = jnp.clip(ac_ref[0, 0, r, k] - HB, 0, rows - 1)
                piece = e_own[col]
                if k == 1:
                    keep = jnp.logical_or(first, i > 0)
                    piece = jnp.where(keep, piece, jnp.zeros_like(piece))
                if k == slots - 1:
                    keep = jnp.logical_or(last, i < rows // GROUP - 1)
                    piece = jnp.where(keep, piece, jnp.zeros_like(piece))
                pieces.append(piece)
            lhs = jnp.concatenate([a_v[r, k] for k in range(slots)], axis=1)
            rhs = jnp.concatenate(pieces, axis=0)
            res = jnp.dot(lhs, rhs, preferred_element_type=F32)
            g_own[pl.ds(pl.multiple_of(r * width, width), width), :] = res.astype(BF)
        return carry

    lax.fori_loop(0, rows // GROUP, multiply, 0)

    def store_term(part, lhs_cols, rhs):
        for c in range(NC):
            res = jnp.dot(
                et[c * width : (c + 1) * width, lhs_cols], rhs[...], preferred_element_type=F32
            )
            for d in range(NC):
                term[c * band + part * NC + d] = res[:, d * width : (d + 1) * width]

    def block_of(s):
        part = (s // (NC * NC) + 1) % 3
        i = s % (NC * NC)
        return (i // NC) * band + part * NC + i % NC

    def up_copy(b, middle):
        return pltpu.make_async_remote_copy(
            src_ref=half.at[b],
            dst_ref=(from_inner if middle else from_outer).at[b],
            send_sem=up_send.at[b],
            recv_sem=(down_recv if middle else up_recv).at[b],
            device_id=(region, inner),
            device_id_type=MESH,
        )

    def down_copy(b):
        return pltpu.make_async_remote_copy(
            src_ref=from_inner.at[b],
            dst_ref=from_inner.at[b],
            send_sem=down_send.at[b],
            recv_sem=down_recv.at[b],
            device_id=(region, outer),
            device_id_type=MESH,
        )

    def out_copy(b):
        return pltpu.make_async_copy(from_inner.at[b], out_ref.at[b], out_sem.at[b])

    def send_up(b):
        @pl.when(is_mid)
        def _():
            up_copy(b, True).start()

        @pl.when(jnp.logical_not(is_mid))
        def _():
            up_copy(b, False).start()

    def up_end(s, carry):
        b = block_of(s)
        half[b] = term[b].astype(BF)
        send_up(b)
        return carry

    def up_pass(s):
        b = block_of(s)
        up_copy(b, False).wait_recv()
        half[b] = (term[b] + from_outer[b].astype(F32)).astype(BF)
        send_up(b)

    def down(s, forward):
        b = block_of(s)
        up_copy(b, True).wait_recv()

        @pl.when(is_mid)
        def _():
            from_inner[b] = (half[b].astype(F32) + from_inner[b].astype(F32)).astype(BF)

        if forward:
            down_copy(b).start()
        out_copy(b).start()

    store_term(1, slice(0, rows * width), g_own)

    @pl.when(is_end)
    def _():
        lax.fori_loop(0, NC * NC, up_end, 0)

    def side(e_side, halo, g_side, there, copy, ids_region, row_at, k, base):
        @pl.when(there)
        def _():
            copy().wait_recv()
            for i in range(HB):
                e_side[i] = placed(
                    halo[i, 0],
                    halo[i, 1],
                    pc_ref[ids_region, 0, (rows - HB + i) if k == 1 else i, 0],
                    pc_ref[ids_region, 0, (rows - HB + i) if k == 1 else i, 1],
                )

        @pl.when(jnp.logical_not(there))
        def _():
            e_side[...] = jnp.zeros_like(e_side)

        for i in range(HB):
            col = jnp.clip(ac_ref[0, 0, row_at + i, k] - base, 0, HB - 1)
            res = jnp.dot(a_v[row_at + i, k], e_side[col], preferred_element_type=F32)
            g_side[i * width : (i + 1) * width, :] = res.astype(BF)

    side(
        e_hi, halo_hi, g_hi, jnp.logical_not(last), to_previous,
        jnp.minimum(region + 1, regions - 1), rows - HB, slots - 1, rows + HB,
    )
    store_term(2, slice((rows - HB) * width, rows * width), g_hi)
    side(
        e_lo, halo_lo, g_lo, jnp.logical_not(first), to_next,
        jnp.maximum(region - 1, 0), 0, 1, 0,
    )
    store_term(0, slice(0, HB * width), g_lo)

    @pl.when(is_end)
    def _():
        lax.fori_loop(NC * NC, count, up_end, 0)

        def step(s, carry):
            down(s, False)
            return carry

        lax.fori_loop(0, count, step, 0)

    @pl.when(has_outer)
    def _():
        def head(s, carry):
            up_pass(s)
            return carry

        def steady(s, carry):
            up_pass(s)
            down(s - LAG, True)
            return carry

        def tail(s, carry):
            down(s, True)
            return carry

        lax.fori_loop(0, LAG, head, 0)
        lax.fori_loop(LAG, count, steady, 0)
        lax.fori_loop(count - LAG, count, tail, 0)

        def sent(b, carry):
            down_copy(b).wait_send()
            return carry

        lax.fori_loop(0, count, sent, 0)

    def drain(b, carry):
        up_copy(b, False).wait_send()
        out_copy(b).wait()
        return carry

    lax.fori_loop(0, count, drain, 0)

    @pl.when(jnp.logical_not(last))
    def _():
        to_next().wait_send()

    @pl.when(jnp.logical_not(first))
    def _():
        to_previous().wait_send()


def body(regions, members, a_blocks, a_cols, p_blocks, p_cols):
    rows, slots = a_blocks.shape[2:4]
    p_slots = p_blocks.shape[3]
    width = a_blocks.shape[-1]
    wide = NC * width
    band = 3 * NC
    count = NC * band
    dma = pltpu.SemaphoreType.DMA
    out = pl.pallas_call(
        functools.partial(kernel, regions, members),
        out_shape=jax.ShapeDtypeStruct((count, width, width), BF),
        in_specs=[
            pl.BlockSpec(memory_space=pl.ANY),
            pl.BlockSpec(memory_space=pltpu.SMEM),
            pl.BlockSpec(memory_space=pl.ANY),
            pl.BlockSpec(memory_space=pltpu.SMEM),
        ],
        out_specs=pl.BlockSpec(memory_space=pl.ANY),
        scratch_shapes=[
            pltpu.VMEM((rows, slots, width, width), BF),
            pltpu.VMEM((rows, p_slots, width, width), BF),
            pltpu.VMEM((HB, p_slots, width, width), BF),
            pltpu.VMEM((HB, p_slots, width, width), BF),
            pltpu.VMEM((rows, width, wide), BF),
            pltpu.VMEM((HB, width, wide), BF),
            pltpu.VMEM((HB, width, wide), BF),
            pltpu.VMEM((wide, rows * width), BF),
            pltpu.VMEM((rows * width, wide), BF),
            pltpu.VMEM((HB * width, wide), BF),
            pltpu.VMEM((HB * width, wide), BF),
            pltpu.VMEM((count, width, width), F32),
            pltpu.VMEM((count, width, width), BF),
            pltpu.VMEM((count, width, width), BF),
            pltpu.VMEM((count, width, width), BF),
            dma((rows // GROUP,)),
            dma,
            dma,
            dma,
            dma,
            dma,
            dma((count,)),
            dma((count,)),
            dma((count,)),
            dma((count,)),
            dma((count,)),
        ],
        compiler_params=pltpu.CompilerParams(
            collective_id=0, has_side_effects=True, vmem_limit_bytes=48 * 1024 * 1024
        ),
        cost_estimate=pl.CostEstimate(
            flops=2_000_000_000, bytes_accessed=5_000_000, transcendentals=0
        ),
    )(a_blocks, a_cols, p_blocks, p_cols)
    return out.reshape(NC, band, width, width).transpose(2, 0, 1, 3)[None]


def solution(mesh):
    return jax.shard_map(
        functools.partial(body, mesh.shape["agg"], mesh.shape["grp"]),
        mesh=mesh,
        in_specs=(
            P("agg", "grp", None, None, None, None),
            P("agg", "grp", None, None),
            P("agg", "grp", None, None, None, None),
            P(None, "grp", None, None),
        ),
        out_specs=P("agg", None, None, None, None),
        check_vma=False,
    )
```

```python
import functools

import jax
import jax.numpy as jnp
from jax import lax
from jax.experimental import pallas as pl
from jax.experimental.pallas import tpu as pltpu
from jax.sharding import PartitionSpec as P

NC = 3
HB = 4
LAG = 4
GROUP = 4
MESH = pl.DeviceIdType.MESH
BF = jnp.bfloat16
F32 = jnp.float32


def kernel(
    regions,
    members,
    a_ref,
    ac_ref,
    p_ref,
    pc_ref,
    out_ref,
    a_v,
    p_v,
    halo_lo,
    halo_hi,
    e_own,
    e_lo,
    e_hi,
    et,
    g_own,
    g_lo,
    g_hi,
    term,
    half,
    from_outer,
    from_inner,
    a_sem,
    p_sem,
    lo_send,
    lo_recv,
    hi_send,
    hi_recv,
    up_send,
    up_recv,
    down_send,
    down_recv,
    out_sem,
):
    rows, slots, width = a_v.shape[0], a_v.shape[1], a_v.shape[2]
    wide = NC * width
    band = 3 * NC
    count = NC * band
    region = lax.axis_index("agg")
    g = lax.axis_index("grp")
    first = region == 0
    last = region == regions - 1
    left = g < members // 2
    inner = jnp.where(left, g + 1, g - 1)
    outer = jnp.where(left, g - 1, g + 1)
    has_outer = jnp.logical_and(g > 0, g < members - 1)
    is_end = jnp.logical_not(has_outer)
    is_mid = jnp.logical_or(g == members // 2 - 1, g == members // 2)

    p_copy = pltpu.make_async_copy(p_ref.at[0, 0], p_v, p_sem)
    p_copy.start()

    def a_copy(i):
        return pltpu.make_async_copy(
            a_ref.at[0, 0, pl.ds(i * GROUP, GROUP)],
            a_v.at[pl.ds(i * GROUP, GROUP)],
            a_sem.at[i],
        )

    for i in range(rows // GROUP):
        a_copy(i).start()

    barrier = pltpu.get_barrier_semaphore()

    def greet(there, agg, grp):
        @pl.when(there)
        def _():
            pl.semaphore_signal(barrier, inc=1, device_id=(agg, grp), device_id_type=MESH)

    greet(jnp.logical_not(first), region - 1, g)
    greet(jnp.logical_not(last), region + 1, g)
    greet(has_outer, region, outer)
    greet(jnp.bool_(True), region, inner)
    def place(block_0, block_1, id_0, id_1, c):
        zero = jnp.zeros_like(block_0)
        return jnp.where(id_0 == c, block_0, jnp.where(id_1 == c, block_1, zero))

    p_copy.wait()

    def build(r, carry):
        for c in range(NC):
            e_own[c, r] = place(
                p_v[r, 0], p_v[r, 1], pc_ref[region, 0, 0, r], pc_ref[region, 0, 1, r], c
            )
        return carry

    lax.fori_loop(0, rows, build, 0, unroll=4)

    pl.semaphore_wait(
        barrier,
        1
        + has_outer.astype(jnp.int32)
        + jnp.logical_not(first).astype(jnp.int32)
        + jnp.logical_not(last).astype(jnp.int32),
    )

    def to_next():
        return pltpu.make_async_remote_copy(
            src_ref=p_ref.at[0, 0, pl.ds(rows - HB, HB)],
            dst_ref=halo_lo,
            send_sem=lo_send,
            recv_sem=lo_recv,
            device_id=(region + 1, g),
            device_id_type=MESH,
        )

    def to_previous():
        return pltpu.make_async_remote_copy(
            src_ref=p_ref.at[0, 0, pl.ds(0, HB)],
            dst_ref=halo_hi,
            send_sem=hi_send,
            recv_sem=hi_recv,
            device_id=(region - 1, g),
            device_id_type=MESH,
        )

    @pl.when(jnp.logical_not(last))
    def _():
        to_next().start()

    @pl.when(jnp.logical_not(first))
    def _():
        to_previous().start()

    def multiply(q):
        def step(i, carry):
            if q == 0:
                a_copy(i).wait()
            for j in range(GROUP):
                r = i * GROUP + j
                here = pl.ds(pl.multiple_of(r * width, width), width)
                pieces = []
                for k in range(slots):
                    col = jnp.clip(ac_ref[0, k, 0, r] - HB, 0, rows - 1)
                    piece = e_own[q, col]
                    if k == 1:
                        keep = jnp.logical_or(first, i > 0)
                        piece = jnp.where(keep, piece, jnp.zeros_like(piece))
                    if k == slots - 1:
                        keep = jnp.logical_or(last, i < rows // GROUP - 1)
                        piece = jnp.where(keep, piece, jnp.zeros_like(piece))
                    pieces.append(piece)
                lhs = jnp.concatenate([a_v[r, k] for k in range(slots)], axis=1)
                rhs = jnp.concatenate(pieces, axis=0)
                res = jnp.dot(lhs, rhs, preferred_element_type=F32)
                g_own[q, here, :] = res.astype(BF)
                if q == 0:
                    turned_0 = p_v[r, 0].T
                    turned_1 = p_v[r, 1].T
                    for c in range(NC):
                        et[c * width : (c + 1) * width, here] = place(
                            turned_0, turned_1, pc_ref[region, 0, 0, r], pc_ref[region, 0, 1, r], c
                        )
            return carry

        lax.fori_loop(0, rows // GROUP, step, 0)

    def own_term(q):
        res = jnp.dot(et[...], g_own[q], preferred_element_type=F32)
        for c in range(NC):
            term[c * band + NC + q] = res[c * width : (c + 1) * width]

    def store_term(part, lhs_cols, rhs):
        for c in range(NC):
            res = jnp.dot(
                et[c * width : (c + 1) * width, lhs_cols], rhs[...], preferred_element_type=F32
            )
            for d in range(NC):
                term[c * band + part * NC + d] = res[:, d * width : (d + 1) * width]

    def block_of(s):
        part = (s // (NC * NC) + 1) % 3
        i = s % (NC * NC)
        return (i % NC) * band + part * NC + i // NC

    def up_copy(b, middle):
        return pltpu.make_async_remote_copy(
            src_ref=half.at[b],
            dst_ref=(from_inner if middle else from_outer).at[b],
            send_sem=up_send.at[b],
            recv_sem=(down_recv if middle else up_recv).at[b],
            device_id=(region, inner),
            device_id_type=MESH,
        )

    def down_copy(b):
        return pltpu.make_async_remote_copy(
            src_ref=from_inner.at[b],
            dst_ref=from_inner.at[b],
            send_sem=down_send.at[b],
            recv_sem=down_recv.at[b],
            device_id=(region, outer),
            device_id_type=MESH,
        )

    def out_copy(b):
        return pltpu.make_async_copy(from_inner.at[b], out_ref.at[b], out_sem.at[b])

    def send_up(b):
        @pl.when(is_mid)
        def _():
            up_copy(b, True).start()

        @pl.when(jnp.logical_not(is_mid))
        def _():
            up_copy(b, False).start()

    def up_end(s, carry):
        b = block_of(s)
        half[b] = term[b].astype(BF)
        send_up(b)
        return carry

    def up_pass(s):
        b = block_of(s)
        up_copy(b, False).wait_recv()
        half[b] = (term[b] + from_outer[b].astype(F32)).astype(BF)
        send_up(b)

    def down(s, forward):
        b = block_of(s)
        up_copy(b, True).wait_recv()

        @pl.when(is_mid)
        def _():
            from_inner[b] = (half[b].astype(F32) + from_inner[b].astype(F32)).astype(BF)

        if forward:
            down_copy(b).start()
        out_copy(b).start()

    def side(e_side, halo, g_side, there, copy, ids_region, row_at, k, base):
        @pl.when(there)
        def _():
            copy().wait_recv()
            for i in range(HB):
                at = (rows - HB + i) if k == 1 else i
                id_0, id_1 = pc_ref[ids_region, 0, 0, at], pc_ref[ids_region, 0, 1, at]
                for c in range(NC):
                    e_side[i, :, c * width : (c + 1) * width] = place(
                        halo[i, 0], halo[i, 1], id_0, id_1, c
                    )

        @pl.when(jnp.logical_not(there))
        def _():
            e_side[...] = jnp.zeros_like(e_side)

        for i in range(HB):
            col = jnp.clip(ac_ref[0, k, 0, row_at + i] - base, 0, HB - 1)
            res = jnp.dot(a_v[row_at + i, k], e_side[col], preferred_element_type=F32)
            g_side[i * width : (i + 1) * width, :] = res.astype(BF)

    def end_up(start, stop):
        @pl.when(is_end)
        def _():
            lax.fori_loop(start, stop, up_end, 0)

    def middle_pass(start, stop, lag):
        @pl.when(has_outer)
        def _():
            def step(s, carry):
                up_pass(s)
                if lag:
                    down(s - lag, True)
                return carry

            lax.fori_loop(start, stop, step, 0)

    own = NC * NC
    multiply(0)
    own_term(0)
    end_up(0, NC)
    multiply(1)
    middle_pass(0, NC, 0)
    own_term(1)
    end_up(NC, 2 * NC)
    multiply(2)
    middle_pass(NC, 2 * NC, 0)
    own_term(2)
    end_up(2 * NC, own)
    middle_pass(2 * NC, own, 2 * NC)
    side(
        e_hi, halo_hi, g_hi, jnp.logical_not(last), to_previous,
        jnp.minimum(region + 1, regions - 1), rows - HB, slots - 1, rows + HB,
    )
    store_term(2, slice((rows - HB) * width, rows * width), g_hi)
    end_up(own, 2 * own)
    middle_pass(own, own + NC, 2 * NC)
    side(
        e_lo, halo_lo, g_lo, jnp.logical_not(first), to_next,
        jnp.maximum(region - 1, 0), 0, 1, 0,
    )
    store_term(0, slice(0, HB * width), g_lo)
    end_up(2 * own, count)
    middle_pass(own + NC, own + NC + 1, 2 * NC)

    @pl.when(is_end)
    def _():
        def step(s, carry):
            down(s, False)
            return carry

        lax.fori_loop(0, count, step, 0)

    @pl.when(has_outer)
    def _():
        at = own + NC + 1

        def catch_up(s, carry):
            down(s, True)
            return carry

        lax.fori_loop(at - 2 * NC, at - LAG, catch_up, 0)

        def steady(s, carry):
            up_pass(s)
            down(s - LAG, True)
            return carry

        lax.fori_loop(at, count, steady, 0)
        lax.fori_loop(count - LAG, count, catch_up, 0)

        def sent(b, carry):
            down_copy(b).wait_send()
            return carry

        lax.fori_loop(0, count, sent, 0)

    def drain(b, carry):
        up_copy(b, False).wait_send()
        out_copy(b).wait()
        return carry

    lax.fori_loop(0, count, drain, 0)

    @pl.when(jnp.logical_not(last))
    def _():
        to_next().wait_send()

    @pl.when(jnp.logical_not(first))
    def _():
        to_previous().wait_send()


def body(regions, members, a_blocks, a_cols, p_blocks, p_cols):
    rows, slots = a_blocks.shape[2:4]
    p_slots = p_blocks.shape[3]
    width = a_blocks.shape[-1]
    wide = NC * width
    band = 3 * NC
    count = NC * band
    dma = pltpu.SemaphoreType.DMA
    out = pl.pallas_call(
        functools.partial(kernel, regions, members),
        out_shape=jax.ShapeDtypeStruct((count, width, width), BF),
        in_specs=[
            pl.BlockSpec(memory_space=pltpu.HBM),
            pl.BlockSpec(memory_space=pltpu.SMEM),
            pl.BlockSpec(memory_space=pltpu.HBM),
            pl.BlockSpec(memory_space=pltpu.SMEM),
        ],
        out_specs=pl.BlockSpec(memory_space=pl.ANY),
        scratch_shapes=[
            pltpu.VMEM((rows, slots, width, width), BF),
            pltpu.VMEM((rows, p_slots, width, width), BF),
            pltpu.VMEM((HB, p_slots, width, width), BF),
            pltpu.VMEM((HB, p_slots, width, width), BF),
            pltpu.VMEM((NC, rows, width, width), BF),
            pltpu.VMEM((HB, width, wide), BF),
            pltpu.VMEM((HB, width, wide), BF),
            pltpu.VMEM((wide, rows * width), BF),
            pltpu.VMEM((NC, rows * width, width), BF),
            pltpu.VMEM((HB * width, wide), BF),
            pltpu.VMEM((HB * width, wide), BF),
            pltpu.VMEM((count, width, width), F32),
            pltpu.VMEM((count, width, width), BF),
            pltpu.VMEM((count, width, width), BF),
            pltpu.VMEM((count, width, width), BF),
            dma((rows // GROUP,)),
            dma,
            dma,
            dma,
            dma,
            dma,
            dma((count,)),
            dma((count,)),
            dma((count,)),
            dma((count,)),
            dma((count,)),
        ],
        compiler_params=pltpu.CompilerParams(
            collective_id=0, has_side_effects=True, vmem_limit_bytes=60 * 1024 * 1024
        ),
        cost_estimate=pl.CostEstimate(
            flops=2_000_000_000, bytes_accessed=5_000_000, transcendentals=0
        ),
    )(a_blocks, a_cols.transpose(0, 3, 1, 2), p_blocks, p_cols.transpose(0, 1, 3, 2))
    return out.reshape(NC, band, width, width).transpose(2, 0, 1, 3)[None]


def solution(mesh):
    return jax.shard_map(
        functools.partial(body, mesh.shape["agg"], mesh.shape["grp"]),
        mesh=mesh,
        in_specs=(
            P("agg", "grp", None, None, None, None),
            P("agg", "grp", None, None),
            P("agg", "grp", None, None, None, None),
            P(None, "grp", None, None),
        ),
        out_specs=P("agg", None, None, None, None),
        check_vma=False,
    )
```

```python
import functools

import jax
import jax.numpy as jnp
from jax import lax
from jax.experimental import pallas as pl
from jax.experimental.pallas import tpu as pltpu
from jax.sharding import PartitionSpec as P

NC = 3
HB = 4
LAG = 3
GROUP = 4
MESH = pl.DeviceIdType.MESH
BF = jnp.bfloat16
F32 = jnp.float32


def kernel(
    regions,
    members,
    a_ref,
    ac_ref,
    p_ref,
    pc_ref,
    out_ref,
    a_v,
    p_v,
    halo_lo,
    halo_hi,
    e_own,
    e_lo,
    e_hi,
    et,
    g_own,
    g_lo,
    g_hi,
    term,
    half,
    from_outer,
    from_inner,
    a_sem,
    p_sem,
    lo_send,
    lo_recv,
    hi_send,
    hi_recv,
    up_send,
    up_recv,
    down_send,
    down_recv,
    out_sem,
):
    rows, slots, width = a_v.shape[0], a_v.shape[1], a_v.shape[2]
    wide = NC * width
    band = 3 * NC
    count = NC * band
    region = lax.axis_index("agg")
    g = lax.axis_index("grp")
    first = region == 0
    last = region == regions - 1
    left = g < members // 2
    inner = jnp.where(left, g + 1, g - 1)
    outer = jnp.where(left, g - 1, g + 1)
    has_outer = jnp.logical_and(g > 0, g < members - 1)
    is_end = jnp.logical_not(has_outer)
    is_mid = jnp.logical_or(g == members // 2 - 1, g == members // 2)

    p_copy = pltpu.make_async_copy(p_ref.at[0, 0], p_v, p_sem)
    p_copy.start()

    def a_copy(i):
        return pltpu.make_async_copy(
            a_ref.at[0, 0, pl.ds(i * GROUP, GROUP)],
            a_v.at[pl.ds(i * GROUP, GROUP)],
            a_sem.at[i],
        )

    for i in range(rows // GROUP):
        a_copy(i).start()

    barrier = pltpu.get_barrier_semaphore()

    def greet(there, agg, grp):
        @pl.when(there)
        def _():
            pl.semaphore_signal(barrier, inc=1, device_id=(agg, grp), device_id_type=MESH)

    greet(jnp.logical_not(first), region - 1, g)
    greet(jnp.logical_not(last), region + 1, g)
    greet(has_outer, region, outer)
    greet(jnp.bool_(True), region, inner)
    def place(block_0, block_1, id_0, id_1, c):
        zero = jnp.zeros_like(block_0)
        return jnp.where(id_0 == c, block_0, jnp.where(id_1 == c, block_1, zero))

    p_copy.wait()

    def build(r, carry):
        for c in range(NC):
            e_own[c, r] = place(
                p_v[r, 0], p_v[r, 1], pc_ref[region, 0, 0, r], pc_ref[region, 0, 1, r], c
            )
        return carry

    lax.fori_loop(0, rows, build, 0, unroll=4)

    pl.semaphore_wait(
        barrier,
        1
        + has_outer.astype(jnp.int32)
        + jnp.logical_not(first).astype(jnp.int32)
        + jnp.logical_not(last).astype(jnp.int32),
    )

    def to_next():
        return pltpu.make_async_remote_copy(
            src_ref=p_ref.at[0, 0, pl.ds(rows - HB, HB)],
            dst_ref=halo_lo,
            send_sem=lo_send,
            recv_sem=lo_recv,
            device_id=(region + 1, g),
            device_id_type=MESH,
        )

    def to_previous():
        return pltpu.make_async_remote_copy(
            src_ref=p_ref.at[0, 0, pl.ds(0, HB)],
            dst_ref=halo_hi,
            send_sem=hi_send,
            recv_sem=hi_recv,
            device_id=(region - 1, g),
            device_id_type=MESH,
        )

    @pl.when(jnp.logical_not(last))
    def _():
        to_next().start()

    @pl.when(jnp.logical_not(first))
    def _():
        to_previous().start()

    def multiply(q, opening, between):
        for i in range(rows // GROUP):
            if opening:
                a_copy(i).wait()
            for r in range(i * GROUP, (i + 1) * GROUP):
                here = slice(r * width, (r + 1) * width)
                pieces = []
                for k in range(slots):
                    col = jnp.clip(ac_ref[0, k, 0, r] - HB, 0, rows - 1)
                    piece = e_own[q, col]
                    if k == 1 and r < HB:
                        piece = jnp.where(first, piece, jnp.zeros_like(piece))
                    if k == slots - 1 and r >= rows - HB:
                        piece = jnp.where(last, piece, jnp.zeros_like(piece))
                    pieces.append(piece)
                lhs = jnp.concatenate([a_v[r, k] for k in range(slots)], axis=1)
                rhs = jnp.concatenate(pieces, axis=0)
                res = jnp.dot(lhs, rhs, preferred_element_type=F32)
                g_own[q, here, :] = res.astype(BF)
                if opening:
                    turned_0 = p_v[r, 0].T
                    turned_1 = p_v[r, 1].T
                    for c in range(NC):
                        et[c * width : (c + 1) * width, here] = place(
                            turned_0, turned_1, pc_ref[region, 0, 0, r], pc_ref[region, 0, 1, r], c
                        )
            between()

    def own_term(q):
        res = jnp.dot(et[...], g_own[q], preferred_element_type=F32)
        for c in range(NC):
            term[c * band + NC + q] = res[c * width : (c + 1) * width]

    def store_term(part, lhs_cols, rhs):
        for c in range(NC):
            res = jnp.dot(
                et[c * width : (c + 1) * width, lhs_cols], rhs[...], preferred_element_type=F32
            )
            for d in range(NC):
                term[c * band + part * NC + d] = res[:, d * width : (d + 1) * width]

    def block_of(s):
        return (s % NC) * band + (s // NC + 2 * NC - 1) % band

    def up_copy(b, middle):
        return pltpu.make_async_remote_copy(
            src_ref=half.at[b],
            dst_ref=(from_inner if middle else from_outer).at[b],
            send_sem=up_send.at[b],
            recv_sem=(down_recv if middle else up_recv).at[b],
            device_id=(region, inner),
            device_id_type=MESH,
        )

    def down_copy(b):
        return pltpu.make_async_remote_copy(
            src_ref=from_inner.at[b],
            dst_ref=from_inner.at[b],
            send_sem=down_send.at[b],
            recv_sem=down_recv.at[b],
            device_id=(region, outer),
            device_id_type=MESH,
        )

    def out_copy(b):
        return pltpu.make_async_copy(from_inner.at[b], out_ref.at[b], out_sem.at[b])

    def send_up(b):
        @pl.when(is_mid)
        def _():
            up_copy(b, True).start()

        @pl.when(jnp.logical_not(is_mid))
        def _():
            up_copy(b, False).start()

    def up_end(s, carry):
        b = block_of(s)
        half[b] = term[b].astype(BF)
        send_up(b)
        return carry

    def up_pass(s):
        b = block_of(s)
        up_copy(b, False).wait_recv()
        half[b] = (term[b] + from_outer[b].astype(F32)).astype(BF)
        send_up(b)

    def down(s, forward):
        b = block_of(s)
        up_copy(b, True).wait_recv()

        @pl.when(is_mid)
        def _():
            from_inner[b] = (half[b].astype(F32) + from_inner[b].astype(F32)).astype(BF)

        if forward:
            down_copy(b).start()
        out_copy(b).start()

    def side(e_side, halo, g_side, there, copy, ids_region, row_at, k, base):
        @pl.when(there)
        def _():
            copy().wait_recv()
            for i in range(HB):
                at = (rows - HB + i) if k == 1 else i
                id_0, id_1 = pc_ref[ids_region, 0, 0, at], pc_ref[ids_region, 0, 1, at]
                for c in range(NC):
                    e_side[i, :, c * width : (c + 1) * width] = place(
                        halo[i, 0], halo[i, 1], id_0, id_1, c
                    )

        @pl.when(jnp.logical_not(there))
        def _():
            e_side[...] = jnp.zeros_like(e_side)

        for i in range(HB):
            col = jnp.clip(ac_ref[0, k, 0, row_at + i] - base, 0, HB - 1)
            res = jnp.dot(a_v[row_at + i, k], e_side[col], preferred_element_type=F32)
            g_side[i * width : (i + 1) * width, :] = res.astype(BF)

    def end_up(start, stop):
        @pl.when(is_end)
        def _():
            lax.fori_loop(start, stop, up_end, 0)

    passed = [0]

    def middle_pass():
        at = passed[0]
        passed[0] += 1

        @pl.when(has_outer)
        def _():
            up_pass(at)
            if at >= LAG:
                down(at - LAG, True)

    own = NC * NC
    multiply(NC - 1, True, lambda: None)
    own_term(NC - 1)
    end_up(0, NC)
    side(
        e_hi, halo_hi, g_hi, jnp.logical_not(last), to_previous,
        jnp.minimum(region + 1, regions - 1), rows - HB, slots - 1, rows + HB,
    )
    middle_pass()
    store_term(2, slice((rows - HB) * width, rows * width), g_hi)
    end_up(NC, NC + own)
    middle_pass()
    middle_pass()
    side(
        e_lo, halo_lo, g_lo, jnp.logical_not(first), to_next,
        jnp.maximum(region - 1, 0), 0, 1, 0,
    )
    middle_pass()
    store_term(0, slice(0, HB * width), g_lo)
    end_up(NC + own, NC + 2 * own)
    middle_pass()
    for q in range(NC - 1):
        multiply(q, False, middle_pass)
        own_term(q)
        end_up(NC + 2 * own + q * NC, 2 * NC + 2 * own + q * NC)
        middle_pass()

    @pl.when(is_end)
    def _():
        def step(s, carry):
            down(s, False)
            return carry

        lax.fori_loop(0, count, step, 0)

    @pl.when(has_outer)
    def _():
        def steady(s, carry):
            up_pass(s)
            down(s - LAG, True)
            return carry

        def tail(s, carry):
            down(s, True)
            return carry

        lax.fori_loop(passed[0], count, steady, 0)
        lax.fori_loop(count - LAG, count, tail, 0)

        def sent(b, carry):
            down_copy(b).wait_send()
            return carry

        lax.fori_loop(0, count, sent, 0)

    def drain(b, carry):
        up_copy(b, False).wait_send()
        out_copy(b).wait()
        return carry

    lax.fori_loop(0, count, drain, 0)

    @pl.when(jnp.logical_not(last))
    def _():
        to_next().wait_send()

    @pl.when(jnp.logical_not(first))
    def _():
        to_previous().wait_send()


def body(regions, members, a_blocks, a_cols, p_blocks, p_cols):
    rows, slots = a_blocks.shape[2:4]
    p_slots = p_blocks.shape[3]
    width = a_blocks.shape[-1]
    wide = NC * width
    band = 3 * NC
    count = NC * band
    dma = pltpu.SemaphoreType.DMA
    out = pl.pallas_call(
        functools.partial(kernel, regions, members),
        out_shape=pltpu.VMEM((count, width, width), BF),
        in_specs=[
            pl.BlockSpec(memory_space=pltpu.HBM),
            pl.BlockSpec(memory_space=pltpu.SMEM),
            pl.BlockSpec(memory_space=pltpu.HBM),
            pl.BlockSpec(memory_space=pltpu.SMEM),
        ],
        out_specs=pl.BlockSpec(memory_space=pltpu.VMEM),
        scratch_shapes=[
            pltpu.VMEM((rows, slots, width, width), BF),
            pltpu.VMEM((rows, p_slots, width, width), BF),
            pltpu.VMEM((HB, p_slots, width, width), BF),
            pltpu.VMEM((HB, p_slots, width, width), BF),
            pltpu.VMEM((NC, rows, width, width), BF),
            pltpu.VMEM((HB, width, wide), BF),
            pltpu.VMEM((HB, width, wide), BF),
            pltpu.VMEM((wide, rows * width), BF),
            pltpu.VMEM((NC, rows * width, width), BF),
            pltpu.VMEM((HB * width, wide), BF),
            pltpu.VMEM((HB * width, wide), BF),
            pltpu.VMEM((count, width, width), F32),
            pltpu.VMEM((count, width, width), BF),
            pltpu.VMEM((count, width, width), BF),
            pltpu.VMEM((count, width, width), BF),
            dma((rows // GROUP,)),
            dma,
            dma,
            dma,
            dma,
            dma,
            dma((count,)),
            dma((count,)),
            dma((count,)),
            dma((count,)),
            dma((count,)),
        ],
        compiler_params=pltpu.CompilerParams(
            collective_id=0, has_side_effects=True, vmem_limit_bytes=57 * 1024 * 1024
        ),
        cost_estimate=pl.CostEstimate(
            flops=2_000_000_000, bytes_accessed=5_000_000, transcendentals=0
        ),
    )(a_blocks, a_cols.transpose(0, 3, 1, 2), p_blocks, p_cols.transpose(0, 1, 3, 2))
    return out.reshape(NC, band, width, width).transpose(2, 0, 1, 3)[None]


def solution(mesh):
    return jax.shard_map(
        functools.partial(body, mesh.shape["agg"], mesh.shape["grp"]),
        mesh=mesh,
        in_specs=(
            P("agg", "grp", None, None, None, None),
            P("agg", "grp", None, None),
            P("agg", "grp", None, None, None, None),
            P(None, "grp", None, None),
        ),
        out_specs=P("agg", None, None, None, None),
        check_vma=False,
    )
```

```python
import functools

import jax
import jax.numpy as jnp
from jax import lax
from jax.experimental import pallas as pl
from jax.experimental.pallas import tpu as pltpu
from jax.sharding import PartitionSpec as P

NC = 3
HB = 4
LAG = 3
GROUP = 4
MESH = pl.DeviceIdType.MESH
BF = jnp.bfloat16
F32 = jnp.float32


def kernel(
    regions,
    members,
    a_ref,
    ac_ref,
    p_ref,
    pc_ref,
    out_ref,
    a_v,
    p_v,
    halo_lo,
    halo_hi,
    e_own,
    e_lo,
    e_hi,
    et,
    g_own,
    g_lo,
    g_hi,
    term,
    half,
    from_outer,
    from_inner,
    a_sem,
    p_sem,
    lo_send,
    lo_recv,
    hi_send,
    hi_recv,
    up_send,
    up_recv,
    down_send,
    down_recv,
    out_sem,
):
    rows, slots, width = a_v.shape[0], a_v.shape[1], a_v.shape[2]
    wide = NC * width
    band = 3 * NC
    count = NC * band
    region = lax.axis_index("agg")
    g = lax.axis_index("grp")
    first = region == 0
    last = region == regions - 1
    left = g < members // 2
    inner = jnp.where(left, g + 1, g - 1)
    outer = jnp.where(left, g - 1, g + 1)
    has_outer = jnp.logical_and(g > 0, g < members - 1)
    is_end = jnp.logical_not(has_outer)
    is_mid = jnp.logical_or(g == members // 2 - 1, g == members // 2)

    p_copy = pltpu.make_async_copy(p_ref.at[0, 0], p_v, p_sem)
    p_copy.start()

    def a_copy(i):
        return pltpu.make_async_copy(
            a_ref.at[0, 0, pl.ds(i * GROUP, GROUP)],
            a_v.at[pl.ds(i * GROUP, GROUP)],
            a_sem.at[i],
        )

    for i in range(rows // GROUP):
        a_copy(i).start()

    barrier = pltpu.get_barrier_semaphore()

    def greet(there, agg, grp):
        @pl.when(there)
        def _():
            pl.semaphore_signal(barrier, inc=1, device_id=(agg, grp), device_id_type=MESH)

    greet(jnp.logical_not(first), region - 1, g)
    greet(jnp.logical_not(last), region + 1, g)
    greet(has_outer, region, outer)
    greet(jnp.bool_(True), region, inner)
    def place(block_0, block_1, id_0, id_1, c):
        zero = jnp.zeros_like(block_0)
        return jnp.where(id_0 == c, block_0, jnp.where(id_1 == c, block_1, zero))

    p_copy.wait()

    def build(r, carry):
        for c in range(NC):
            e_own[c, r] = place(
                p_v[r, 0], p_v[r, 1], pc_ref[region, 0, 0, r], pc_ref[region, 0, 1, r], c
            )
        return carry

    lax.fori_loop(0, rows, build, 0, unroll=4)

    pl.semaphore_wait(
        barrier,
        1
        + has_outer.astype(jnp.int32)
        + jnp.logical_not(first).astype(jnp.int32)
        + jnp.logical_not(last).astype(jnp.int32),
    )

    def to_next(i):
        return pltpu.make_async_remote_copy(
            src_ref=p_ref.at[0, 0, rows - HB + i],
            dst_ref=halo_lo.at[i],
            send_sem=lo_send.at[i],
            recv_sem=lo_recv.at[i],
            device_id=(region + 1, g),
            device_id_type=MESH,
        )

    def to_previous(i):
        return pltpu.make_async_remote_copy(
            src_ref=p_ref.at[0, 0, i],
            dst_ref=halo_hi.at[i],
            send_sem=hi_send.at[i],
            recv_sem=hi_recv.at[i],
            device_id=(region - 1, g),
            device_id_type=MESH,
        )

    @pl.when(jnp.logical_not(first))
    def _():
        for i in range(HB):
            to_previous(i).start()

    @pl.when(jnp.logical_not(last))
    def _():
        for i in range(HB):
            to_next(i).start()

    def multiply(q, opening, between):
        for i in range(rows // GROUP):
            if opening:
                a_copy(i).wait()
            for r in range(i * GROUP, (i + 1) * GROUP):
                here = slice(r * width, (r + 1) * width)
                pieces = []
                for k in range(slots):
                    col = jnp.clip(ac_ref[0, k, 0, r] - HB, 0, rows - 1)
                    piece = e_own[q, col]
                    if k == 1 and r < HB:
                        piece = jnp.where(first, piece, jnp.zeros_like(piece))
                    if k == slots - 1 and r >= rows - HB:
                        piece = jnp.where(last, piece, jnp.zeros_like(piece))
                    pieces.append(piece)
                lhs = jnp.concatenate([a_v[r, k] for k in range(slots)], axis=1)
                rhs = jnp.concatenate(pieces, axis=0)
                res = jnp.dot(lhs, rhs, preferred_element_type=F32)
                g_own[q, here, :] = res.astype(BF)
                if opening:
                    turned_0 = p_v[r, 0].T
                    turned_1 = p_v[r, 1].T
                    for c in range(NC):
                        et[c * width : (c + 1) * width, here] = place(
                            turned_0, turned_1, pc_ref[region, 0, 0, r], pc_ref[region, 0, 1, r], c
                        )
            between(i)

    def own_term(q):
        res = jnp.dot(et[...], g_own[q], preferred_element_type=F32)
        for c in range(NC):
            term[c * band + NC + q] = res[c * width : (c + 1) * width]

    def store_term(part, lhs_cols, rhs):
        for c in range(NC):
            res = jnp.dot(
                et[c * width : (c + 1) * width, lhs_cols], rhs[...], preferred_element_type=F32
            )
            for d in range(NC):
                term[c * band + part * NC + d] = res[:, d * width : (d + 1) * width]

    def block_of(s):
        return (s % NC) * band + (s // NC + NC) % band

    def up_copy(b, middle):
        return pltpu.make_async_remote_copy(
            src_ref=half.at[b],
            dst_ref=(from_inner if middle else from_outer).at[b],
            send_sem=up_send.at[b],
            recv_sem=(down_recv if middle else up_recv).at[b],
            device_id=(region, inner),
            device_id_type=MESH,
        )

    def down_copy(b):
        return pltpu.make_async_remote_copy(
            src_ref=from_inner.at[b],
            dst_ref=from_inner.at[b],
            send_sem=down_send.at[b],
            recv_sem=down_recv.at[b],
            device_id=(region, outer),
            device_id_type=MESH,
        )

    def out_copy(b):
        return pltpu.make_async_copy(from_inner.at[b], out_ref.at[b], out_sem.at[b])

    def send_up(b):
        @pl.when(is_mid)
        def _():
            up_copy(b, True).start()

        @pl.when(jnp.logical_not(is_mid))
        def _():
            up_copy(b, False).start()

    def up_end(s, carry):
        b = block_of(s)
        half[b] = term[b].astype(BF)
        send_up(b)
        return carry

    def up_pass(s):
        b = block_of(s)
        up_copy(b, False).wait_recv()
        half[b] = (term[b] + from_outer[b].astype(F32)).astype(BF)
        send_up(b)

    def down(s, forward):
        b = block_of(s)
        up_copy(b, True).wait_recv()

        @pl.when(is_mid)
        def _():
            from_inner[b] = (half[b].astype(F32) + from_inner[b].astype(F32)).astype(BF)

        if forward:
            down_copy(b).start()
        out_copy(b).start()

    def side(e_side, halo, g_side, there, copy, ids_region, row_at, k, base):
        @pl.when(there)
        def _():
            for i in range(HB):
                copy(i).wait_recv()
                at = (rows - HB + i) if k == 1 else i
                id_0, id_1 = pc_ref[ids_region, 0, 0, at], pc_ref[ids_region, 0, 1, at]
                for c in range(NC):
                    e_side[i, :, c * width : (c + 1) * width] = place(
                        halo[i, 0], halo[i, 1], id_0, id_1, c
                    )

        @pl.when(jnp.logical_not(there))
        def _():
            e_side[...] = jnp.zeros_like(e_side)

        for i in range(HB):
            col = jnp.clip(ac_ref[0, k, 0, row_at + i] - base, 0, HB - 1)
            res = jnp.dot(a_v[row_at + i, k], e_side[col], preferred_element_type=F32)
            g_side[i * width : (i + 1) * width, :] = res.astype(BF)

    def end_up(start, stop):
        @pl.when(is_end)
        def _():
            lax.fori_loop(start, stop, up_end, 0)

    passed = [0]

    def middle_pass():
        at = passed[0]
        passed[0] += 1

        @pl.when(has_outer)
        def _():
            up_pass(at)
            if at >= LAG:
                down(at - LAG, True)

    own = NC * NC
    groups = rows // GROUP

    def second(i):
        if i >= groups - 2:
            middle_pass()
        if i == groups - 1:
            middle_pass()

    def third(i):
        if i > 0:
            middle_pass()

    between = [lambda i: None, second, third]
    for q in range(NC):
        multiply(q, q == 0, between[q])
        own_term(q)
        end_up(q * NC, (q + 1) * NC)
    middle_pass()
    middle_pass()
    side(
        e_hi, halo_hi, g_hi, jnp.logical_not(last), to_previous,
        jnp.minimum(region + 1, regions - 1), rows - HB, slots - 1, rows + HB,
    )
    middle_pass()
    store_term(2, slice((rows - HB) * width, rows * width), g_hi)
    end_up(own, 2 * own)
    middle_pass()
    middle_pass()
    side(
        e_lo, halo_lo, g_lo, jnp.logical_not(first), to_next,
        jnp.maximum(region - 1, 0), 0, 1, 0,
    )
    middle_pass()
    store_term(0, slice(0, HB * width), g_lo)
    end_up(2 * own, count)

    @pl.when(is_end)
    def _():
        def step(s, carry):
            down(s, False)
            return carry

        lax.fori_loop(0, count, step, 0)

    @pl.when(has_outer)
    def _():
        def steady(s, carry):
            up_pass(s)
            down(s - LAG, True)
            return carry

        def tail(s, carry):
            down(s, True)
            return carry

        lax.fori_loop(passed[0], count, steady, 0)
        lax.fori_loop(count - LAG, count, tail, 0)

        def sent(b, carry):
            down_copy(b).wait_send()
            return carry

        lax.fori_loop(0, count, sent, 0)

    def drain(b, carry):
        up_copy(b, False).wait_send()
        out_copy(b).wait()
        return carry

    lax.fori_loop(0, count, drain, 0)

    @pl.when(jnp.logical_not(last))
    def _():
        for i in range(HB):
            to_next(i).wait_send()

    @pl.when(jnp.logical_not(first))
    def _():
        for i in range(HB):
            to_previous(i).wait_send()


def body(regions, members, a_blocks, a_cols, p_blocks, p_cols):
    rows, slots = a_blocks.shape[2:4]
    p_slots = p_blocks.shape[3]
    width = a_blocks.shape[-1]
    wide = NC * width
    band = 3 * NC
    count = NC * band
    dma = pltpu.SemaphoreType.DMA
    out = pl.pallas_call(
        functools.partial(kernel, regions, members),
        out_shape=pltpu.VMEM((count, width, width), BF),
        in_specs=[
            pl.BlockSpec(memory_space=pltpu.HBM),
            pl.BlockSpec(memory_space=pltpu.SMEM),
            pl.BlockSpec(memory_space=pltpu.HBM),
            pl.BlockSpec(memory_space=pltpu.SMEM),
        ],
        out_specs=pl.BlockSpec(memory_space=pltpu.VMEM),
        scratch_shapes=[
            pltpu.VMEM((rows, slots, width, width), BF),
            pltpu.VMEM((rows, p_slots, width, width), BF),
            pltpu.VMEM((HB, p_slots, width, width), BF),
            pltpu.VMEM((HB, p_slots, width, width), BF),
            pltpu.VMEM((NC, rows, width, width), BF),
            pltpu.VMEM((HB, width, wide), BF),
            pltpu.VMEM((HB, width, wide), BF),
            pltpu.VMEM((wide, rows * width), BF),
            pltpu.VMEM((NC, rows * width, width), BF),
            pltpu.VMEM((HB * width, wide), BF),
            pltpu.VMEM((HB * width, wide), BF),
            pltpu.VMEM((count, width, width), F32),
            pltpu.VMEM((count, width, width), BF),
            pltpu.VMEM((count, width, width), BF),
            pltpu.VMEM((count, width, width), BF),
            dma((rows // GROUP,)),
            dma,
            dma((HB,)),
            dma((HB,)),
            dma((HB,)),
            dma((HB,)),
            dma((count,)),
            dma((count,)),
            dma((count,)),
            dma((count,)),
            dma((count,)),
        ],
        compiler_params=pltpu.CompilerParams(
            collective_id=0, has_side_effects=True, vmem_limit_bytes=57 * 1024 * 1024
        ),
        cost_estimate=pl.CostEstimate(
            flops=2_000_000_000, bytes_accessed=5_000_000, transcendentals=0
        ),
    )(a_blocks, a_cols.transpose(0, 3, 1, 2), p_blocks, p_cols.transpose(0, 1, 3, 2))
    return out.reshape(NC, band, width, width).transpose(2, 0, 1, 3)[None]


def solution(mesh):
    return jax.shard_map(
        functools.partial(body, mesh.shape["agg"], mesh.shape["grp"]),
        mesh=mesh,
        in_specs=(
            P("agg", "grp", None, None, None, None),
            P("agg", "grp", None, None),
            P("agg", "grp", None, None, None, None),
            P(None, "grp", None, None),
        ),
        out_specs=P("agg", None, None, None, None),
        check_vma=False,
    )
```

```python
import functools

import jax
import jax.numpy as jnp
from jax import lax
from jax.experimental import pallas as pl
from jax.experimental.pallas import tpu as pltpu
from jax.sharding import PartitionSpec as P

NC = 3
HB = 4
LAG = 4
GROUP = 4
MESH = pl.DeviceIdType.MESH
BF = jnp.bfloat16
F32 = jnp.float32


def kernel(
    regions,
    members,
    a_ref,
    ac_ref,
    p_ref,
    pc_ref,
    out_ref,
    a_v,
    p_v,
    halo_lo,
    halo_hi,
    e_own,
    e_lo,
    e_hi,
    et,
    g_own,
    g_lo,
    g_hi,
    term,
    half,
    from_outer,
    from_inner,
    a_sem,
    p_sem,
    lo_send,
    lo_recv,
    hi_send,
    hi_recv,
    up_send,
    up_recv,
    down_send,
    down_recv,
    out_sem,
):
    rows, slots, width = a_v.shape[0], a_v.shape[1], a_v.shape[2]
    wide = NC * width
    band = 3 * NC
    count = NC * band
    region = lax.axis_index("agg")
    g = lax.axis_index("grp")
    first = region == 0
    last = region == regions - 1
    left = g < members // 2
    inner = jnp.where(left, g + 1, g - 1)
    outer = jnp.where(left, g - 1, g + 1)
    has_outer = jnp.logical_and(g > 0, g < members - 1)
    is_end = jnp.logical_not(has_outer)
    is_mid = jnp.logical_or(g == members // 2 - 1, g == members // 2)

    p_copy = pltpu.make_async_copy(p_ref.at[0, 0], p_v, p_sem)
    p_copy.start()

    def a_copy(i):
        return pltpu.make_async_copy(
            a_ref.at[0, 0, pl.ds(i * GROUP, GROUP)],
            a_v.at[pl.ds(i * GROUP, GROUP)],
            a_sem.at[i],
        )

    for i in range(rows // GROUP):
        a_copy(i).start()

    barrier = pltpu.get_barrier_semaphore()

    def greet(there, agg, grp):
        @pl.when(there)
        def _():
            pl.semaphore_signal(barrier, inc=1, device_id=(agg, grp), device_id_type=MESH)

    greet(jnp.logical_not(first), region - 1, g)
    greet(jnp.logical_not(last), region + 1, g)
    greet(has_outer, region, outer)
    greet(jnp.bool_(True), region, inner)
    def place(block_0, block_1, id_0, id_1, c):
        zero = jnp.zeros_like(block_0)
        return jnp.where(id_0 == c, block_0, jnp.where(id_1 == c, block_1, zero))

    p_copy.wait()

    def build(r, carry):
        for c in range(NC):
            e_own[c, r] = place(
                p_v[r, 0], p_v[r, 1], pc_ref[region, 0, 0, r], pc_ref[region, 0, 1, r], c
            )
        return carry

    lax.fori_loop(0, rows, build, 0, unroll=4)

    pl.semaphore_wait(
        barrier,
        1
        + has_outer.astype(jnp.int32)
        + jnp.logical_not(first).astype(jnp.int32)
        + jnp.logical_not(last).astype(jnp.int32),
    )

    def to_next():
        return pltpu.make_async_remote_copy(
            src_ref=p_ref.at[0, 0, pl.ds(rows - HB, HB)],
            dst_ref=halo_lo,
            send_sem=lo_send,
            recv_sem=lo_recv,
            device_id=(region + 1, g),
            device_id_type=MESH,
        )

    def to_previous():
        return pltpu.make_async_remote_copy(
            src_ref=p_ref.at[0, 0, pl.ds(0, HB)],
            dst_ref=halo_hi,
            send_sem=hi_send,
            recv_sem=hi_recv,
            device_id=(region - 1, g),
            device_id_type=MESH,
        )

    @pl.when(jnp.logical_not(last))
    def _():
        to_next().start()

    @pl.when(jnp.logical_not(first))
    def _():
        to_previous().start()

    def multiply(q):
        def step(i, carry):
            if q == 0:
                a_copy(i).wait()
            for j in range(GROUP):
                r = i * GROUP + j
                here = pl.ds(pl.multiple_of(r * width, width), width)
                pieces = []
                for k in range(slots):
                    col = jnp.clip(ac_ref[0, k, 0, r] - HB, 0, rows - 1)
                    piece = e_own[q, col]
                    if k == 1:
                        keep = jnp.logical_or(first, i > 0)
                        piece = jnp.where(keep, piece, jnp.zeros_like(piece))
                    if k == slots - 1:
                        keep = jnp.logical_or(last, i < rows // GROUP - 1)
                        piece = jnp.where(keep, piece, jnp.zeros_like(piece))
                    pieces.append(piece)
                lhs = jnp.concatenate([a_v[r, k] for k in range(slots)], axis=1)
                rhs = jnp.concatenate(pieces, axis=0)
                res = jnp.dot(lhs, rhs, preferred_element_type=F32)
                g_own[q, here, :] = res.astype(BF)
                if q == 0:
                    turned_0 = p_v[r, 0].T
                    turned_1 = p_v[r, 1].T
                    for c in range(NC):
                        et[c * width : (c + 1) * width, here] = place(
                            turned_0, turned_1, pc_ref[region, 0, 0, r], pc_ref[region, 0, 1, r], c
                        )
            return carry

        lax.fori_loop(0, rows // GROUP, step, 0)

    def own_term(q):
        res = jnp.dot(et[...], g_own[q], preferred_element_type=F32)
        for c in range(NC):
            term[c * band + NC + q] = res[c * width : (c + 1) * width]

    def store_term(part, lhs_cols, rhs):
        for c in range(NC):
            res = jnp.dot(
                et[c * width : (c + 1) * width, lhs_cols], rhs[...], preferred_element_type=F32
            )
            for d in range(NC):
                term[c * band + part * NC + d] = res[:, d * width : (d + 1) * width]

    def block_of(s):
        part = (s // (NC * NC) + 1) % 3
        i = s % (NC * NC)
        return (i % NC) * band + part * NC + i // NC

    def up_copy(b, middle):
        return pltpu.make_async_remote_copy(
            src_ref=half.at[b],
            dst_ref=(from_inner if middle else from_outer).at[b],
            send_sem=up_send.at[b],
            recv_sem=(down_recv if middle else up_recv).at[b],
            device_id=(region, inner),
            device_id_type=MESH,
        )

    def down_copy(b):
        return pltpu.make_async_remote_copy(
            src_ref=from_inner.at[b],
            dst_ref=from_inner.at[b],
            send_sem=down_send.at[b],
            recv_sem=down_recv.at[b],
            device_id=(region, outer),
            device_id_type=MESH,
        )

    def out_copy(b):
        return pltpu.make_async_copy(from_inner.at[b], out_ref.at[b], out_sem.at[b])

    def send_up(b):
        @pl.when(is_mid)
        def _():
            up_copy(b, True).start()

        @pl.when(jnp.logical_not(is_mid))
        def _():
            up_copy(b, False).start()

    def up_end(s, carry):
        b = block_of(s)
        half[b] = term[b].astype(BF)
        send_up(b)
        return carry

    def up_pass(s):
        b = block_of(s)
        up_copy(b, False).wait_recv()
        half[b] = (term[b] + from_outer[b].astype(F32)).astype(BF)
        send_up(b)

    def down(s, forward):
        b = block_of(s)
        up_copy(b, True).wait_recv()

        @pl.when(is_mid)
        def _():
            from_inner[b] = (half[b].astype(F32) + from_inner[b].astype(F32)).astype(BF)

        if forward:
            down_copy(b).start()
        out_copy(b).start()

    def side(e_side, halo, g_side, there, copy, ids_region, row_at, k, base):
        @pl.when(there)
        def _():
            copy().wait_recv()
            for i in range(HB):
                at = (rows - HB + i) if k == 1 else i
                id_0, id_1 = pc_ref[ids_region, 0, 0, at], pc_ref[ids_region, 0, 1, at]
                for c in range(NC):
                    e_side[i, :, c * width : (c + 1) * width] = place(
                        halo[i, 0], halo[i, 1], id_0, id_1, c
                    )

        @pl.when(jnp.logical_not(there))
        def _():
            e_side[...] = jnp.zeros_like(e_side)

        for i in range(HB):
            col = jnp.clip(ac_ref[0, k, 0, row_at + i] - base, 0, HB - 1)
            res = jnp.dot(a_v[row_at + i, k], e_side[col], preferred_element_type=F32)
            g_side[i * width : (i + 1) * width, :] = res.astype(BF)

    def end_up(start, stop):
        @pl.when(is_end)
        def _():
            lax.fori_loop(start, stop, up_end, 0)

    def middle_pass(start, stop, lag):
        @pl.when(has_outer)
        def _():
            def step(s, carry):
                up_pass(s)
                if lag:
                    down(s - lag, True)
                return carry

            lax.fori_loop(start, stop, step, 0)

    own = NC * NC
    multiply(0)
    own_term(0)
    end_up(0, NC)
    multiply(1)
    middle_pass(0, NC, 0)
    own_term(1)
    end_up(NC, 2 * NC)
    multiply(2)
    middle_pass(NC, 2 * NC, NC)
    own_term(2)
    end_up(2 * NC, own)
    middle_pass(2 * NC, own, NC)
    side(
        e_hi, halo_hi, g_hi, jnp.logical_not(last), to_previous,
        jnp.minimum(region + 1, regions - 1), rows - HB, slots - 1, rows + HB,
    )
    store_term(2, slice((rows - HB) * width, rows * width), g_hi)
    end_up(own, 2 * own)
    middle_pass(own, own + NC, NC)
    side(
        e_lo, halo_lo, g_lo, jnp.logical_not(first), to_next,
        jnp.maximum(region - 1, 0), 0, 1, 0,
    )
    store_term(0, slice(0, HB * width), g_lo)
    end_up(2 * own, count)
    middle_pass(own + NC, own + LAG, 0)

    @pl.when(is_end)
    def _():
        def step(s, carry):
            down(s, False)
            return carry

        lax.fori_loop(0, count, step, 0)

    @pl.when(has_outer)
    def _():
        def steady(s, carry):
            up_pass(s)
            down(s - LAG, True)
            return carry

        def tail(s, carry):
            down(s, True)
            return carry

        lax.fori_loop(own + LAG, count, steady, 0)
        lax.fori_loop(count - LAG, count, tail, 0)

        def sent(b, carry):
            down_copy(b).wait_send()
            return carry

        lax.fori_loop(0, count, sent, 0)

    def drain(b, carry):
        up_copy(b, False).wait_send()
        out_copy(b).wait()
        return carry

    lax.fori_loop(0, count, drain, 0)

    @pl.when(jnp.logical_not(last))
    def _():
        to_next().wait_send()

    @pl.when(jnp.logical_not(first))
    def _():
        to_previous().wait_send()


def body(regions, members, a_blocks, a_cols, p_blocks, p_cols):
    rows, slots = a_blocks.shape[2:4]
    p_slots = p_blocks.shape[3]
    width = a_blocks.shape[-1]
    wide = NC * width
    band = 3 * NC
    count = NC * band
    dma = pltpu.SemaphoreType.DMA
    out = pl.pallas_call(
        functools.partial(kernel, regions, members),
        out_shape=pltpu.VMEM((count, width, width), BF),
        in_specs=[
            pl.BlockSpec(memory_space=pltpu.HBM),
            pl.BlockSpec(memory_space=pltpu.SMEM),
            pl.BlockSpec(memory_space=pltpu.HBM),
            pl.BlockSpec(memory_space=pltpu.SMEM),
        ],
        out_specs=pl.BlockSpec(memory_space=pltpu.VMEM),
        scratch_shapes=[
            pltpu.VMEM((rows, slots, width, width), BF),
            pltpu.VMEM((rows, p_slots, width, width), BF),
            pltpu.VMEM((HB, p_slots, width, width), BF),
            pltpu.VMEM((HB, p_slots, width, width), BF),
            pltpu.VMEM((NC, rows, width, width), BF),
            pltpu.VMEM((HB, width, wide), BF),
            pltpu.VMEM((HB, width, wide), BF),
            pltpu.VMEM((wide, rows * width), BF),
            pltpu.VMEM((NC, rows * width, width), BF),
            pltpu.VMEM((HB * width, wide), BF),
            pltpu.VMEM((HB * width, wide), BF),
            pltpu.VMEM((count, width, width), F32),
            pltpu.VMEM((count, width, width), BF),
            pltpu.VMEM((count, width, width), BF),
            pltpu.VMEM((count, width, width), BF),
            dma((rows // GROUP,)),
            dma,
            dma,
            dma,
            dma,
            dma,
            dma((count,)),
            dma((count,)),
            dma((count,)),
            dma((count,)),
            dma((count,)),
        ],
        compiler_params=pltpu.CompilerParams(
            collective_id=0, has_side_effects=True, vmem_limit_bytes=57 * 1024 * 1024
        ),
        cost_estimate=pl.CostEstimate(
            flops=2_000_000_000, bytes_accessed=5_000_000, transcendentals=0
        ),
    )(a_blocks, a_cols.transpose(0, 3, 1, 2), p_blocks, p_cols.transpose(0, 1, 3, 2))
    return out.reshape(NC, band, width, width).transpose(2, 0, 1, 3)[None]


def solution(mesh):
    return jax.shard_map(
        functools.partial(body, mesh.shape["agg"], mesh.shape["grp"]),
        mesh=mesh,
        in_specs=(
            P("agg", "grp", None, None, None, None),
            P("agg", "grp", None, None),
            P("agg", "grp", None, None, None, None),
            P(None, "grp", None, None),
        ),
        out_specs=P("agg", None, None, None, None),
        check_vma=False,
    )
```
